128 devices in a mesh: frame: 8 (over y, core), elem: 16 (over x, z).
Axes of the slice: x: 4, y: 4, z: 4, core: 2. Of those that a mesh axis runs over, the one named last changes fastest.
Arguments:
- strain_db: bfloat16 [8, 2048, 25, 6, 256], P('frame', 'elem'), may hold values from -6 to 6
- owner: int32 [8, 16384, 1], P(None, ('frame', 'elem')), may hold values from 0 to 15; in each aligned block of 128 rows (0 to 127, 128 to 255, ..., all dimensions but the last counted through in order) at most 12 rows name the same one
- local_elem: int32 [8, 16384], P(None, ('frame', 'elem')), may hold values from 0 to 127
- lattice: int32 [8, 2, 16384], P(None, None, ('frame', 'elem')), may hold values from 0 to 64
- pair_source: int32 [16], replicated, may hold values from 0 to 3
- pair_receiver: int32 [16], replicated, may hold values from 0 to 3
- filters: float32 [64, 64], replicated, may hold values from 0 to 1
Outputs:
- kernel: float32 [16, 64, 16384], P(None, None, ('frame', 'elem'))
The draws below stay inside these ranges and needn't reach their ends.
Inputs may be any that keep to these rules, and one draw needn't show every extreme that they name: `owner`: within one group, the cells of one device name any elem index at most 12 times, and some index reaches that.
All inputs are finite; a program needn't handle non-finite values.
Results may differ from the reference program's by a relative error of at most 0.0068.
Values may be sent and summed in bfloat16 or wider, within the bound.
A program may use at most 128 MiB of HBM per device.

```python
import math
import jax
import jax.numpy as jnp
import numpy as np
from jax import lax

C = 6
NGLL = 5
T_SIZE = 256
NF = 64
FILT = 64
Q = 64
E_DEV = 128
CELL_DEV = 128
GROUPS = 8
HALF = 4
PAIRS = 16
ELEMS = 2048
CELLS = 16384
CAP = 12
N_FRAME = 8
N_ELEM = 16


def place_ends(result, stream_key, smallest, largest):
    place = [jax.random.randint(jax.random.fold_in(stream_key, axis), (), 0, length) for axis, length in enumerate(result.shape)]
    longest = result.shape.index(max(result.shape))
    next_to = place[:longest] + [(place[longest] + 1) % result.shape[longest]] + place[longest + 1:]
    return result.at[tuple(place)].set(smallest).at[tuple(next_to)].set(largest)


def steps_of(rng, dims, pieces, smallest, largest):
    gain = 1.0
    for position, parts in pieces:
        heights = jax.random.uniform(jax.random.fold_in(jax.random.fold_in(rng, 6), position), (parts,), jnp.float32, smallest / len(pieces), largest / len(pieces))
        gain = gain * jnp.repeat(jnp.exp(heights), dims[position] // parts).reshape((-1,) + (1,) * (len(dims) - 1 - position))
    return gain


def rank_table(amount, lean):
    portions = [(1 << 20) // math.isqrt(rank ** lean) + 1 for rank in range(1, amount + 1)]
    spread = 1 + sum(portions) // (1 << 30)
    return np.cumsum(np.array([max(1, weight // spread) for weight in portions]))


def ranked_ids(stream_key, extent, count, skew):
    grid = rank_table(count, skew)
    ticket = jax.random.randint(jax.random.fold_in(stream_key, 1), extent, 0, int(grid[count - 1]))
    rank = jnp.searchsorted(jnp.asarray(grid, jnp.int32), ticket, side="right")
    return jax.random.permutation(jax.random.fold_in(stream_key, 2), count)[rank].astype(jnp.int32)


def assign_block(rng, own, number, rows, count, top, bound, lean):
    order = jax.random.permutation(rng, count)
    crowded, ordinary = shares(count, rows * top, bound, lean, True), shares(count, rows * top, bound, lean, False)
    places = jnp.arange(count)

    def named(sizes, rotation):
        used = int((sizes > 0).sum())
        fixed = max(1, used // 4)
        moved = fixed + (places - fixed + rotation * (used - fixed)) % max(1, count - fixed)
        return jnp.zeros((count,), jnp.int32).at[order[jnp.where(places < fixed, places, moved)]].set(jnp.asarray(sizes, jnp.int32))

    sizes = jnp.where(number % 4 == 0, named(crowded, number // 4), named(ordinary, number - number // 4 - 1))
    mixed = jax.random.permutation(jax.random.fold_in(own, 3), count)
    source_of, taker = mixed[0:count // 2 * 2:2], mixed[1:count // 2 * 2:2]
    slack = jnp.minimum(sizes[source_of] - 1, bound - sizes[taker]) // 2
    slack = jnp.where((source_of == order[0]) | (taker == order[0]) | (sizes[taker] == 0), 0, jnp.maximum(slack, 0))
    moved = jax.random.randint(jax.random.fold_in(own, 4), (count // 2,), 0, 1 << 20) % (slack + 1)
    sizes = sizes.at[source_of].add(-moved).at[taker].add(moved)
    labels = jnp.searchsorted(jnp.cumsum(sizes), jnp.arange(rows * top), side="right").astype(jnp.int32)
    table = labels.reshape(top, rows).T
    table = table[jax.random.permutation(jax.random.fold_in(own, 1), rows)]
    rotation = jax.random.randint(jax.random.fold_in(own, 2), (rows, 1), 0, top)
    return jnp.take_along_axis(table, (jnp.arange(top)[None, :] + rotation) % top, axis=1)


def shares(number_of, total, limit, lean, full):
    weights = [(1 << 20) // math.isqrt(rank ** lean) + 1 for rank in range(1, number_of + 1)]
    largest = limit if full else min(limit, max(-(-total // number_of), total * weights[0] // sum(weights)))
    least = 1 if total - largest >= number_of - 1 else 0
    given, rest = [largest] + [least] * (number_of - 1), total - largest - least * (number_of - 1)
    while rest > 0:
        free = [i for i in range(1, number_of) if given[i] < largest] or [i for i in range(1, number_of) if given[i] < limit]
        mass, remaining = sum([weights[i] for i in free]), rest
        for i in free:
            more = min(limit - given[i], max(1, remaining * weights[i] // mass), rest)
            given[i] = given[i] + more
            rest = rest - more
    return np.array(given)


def normal_values(stream_key, extent, deviation, bound, split=(), kind=jnp.bfloat16):
    entries = deviation * jax.random.normal(stream_key, extent, jnp.float32)
    if split:
        entries = entries * steps_of(stream_key, extent, split, -0.22, 0.18)
    return jnp.clip(entries, -bound, bound).astype(kind)


def setup_inputs(seed: int = 0) -> dict:
    streams_of = jax.random.split(jax.random.key(seed), 8)
    strain_db = normal_values(streams_of[0], (GROUPS, ELEMS, NGLL * NGLL, C, T_SIZE), 1.0, 6.0, ((0, 8), (1, 16)))
    owner_keys = jax.random.split(jax.random.fold_in(streams_of[1], 1), GROUPS * CELLS // CELL_DEV)
    owner_turns = jax.random.permutation(jax.random.fold_in(streams_of[1], 3), GROUPS * CELLS // CELL_DEV)
    owner = jax.vmap(lambda own, number: assign_block(jax.random.fold_in(streams_of[1], 2), own, number, CELL_DEV, N_ELEM, 1, CAP, 2))(owner_keys, owner_turns).reshape((GROUPS, CELLS, 1))
    local_elem = place_ends(ranked_ids(streams_of[2], (GROUPS, CELLS), E_DEV, 2), jax.random.fold_in(streams_of[2], 3), 0, E_DEV - 1).astype(jnp.int32)
    lattice = place_ends(jax.random.randint(streams_of[3], (GROUPS, 2, CELLS), 0, Q + 1), jax.random.fold_in(streams_of[3], 1), 0, Q).astype(jnp.int32)
    pair_source = place_ends(jax.random.randint(streams_of[4], (PAIRS,), 0, HALF), jax.random.fold_in(streams_of[4], 1), 0, HALF - 1).astype(jnp.int32)
    pair_receiver = place_ends(jax.random.randint(streams_of[5], (PAIRS,), 0, HALF), jax.random.fold_in(streams_of[5], 1), 0, HALF - 1).astype(jnp.int32)
    filters = jnp.clip(jax.random.uniform(streams_of[6], (FILT, NF), jnp.float32, 0.0, 1.0), 0.0, 1.0)
    return dict(strain_db=strain_db, owner=owner, local_elem=local_elem, lattice=lattice, pair_source=pair_source, pair_receiver=pair_receiver, filters=filters)


gll_nodes = [-1.0, -math.sqrt(3.0 / 7.0), 0.0, math.sqrt(3.0 / 7.0), 1.0]

def lagrange(coord):
    values = []
    for i in range(5):
        term = jnp.ones_like(coord)
        for j in range(5):
            if j != i:
                term = term * (coord - gll_nodes[j]) / (gll_nodes[i] - gll_nodes[j])
        values.append(term)
    return jnp.stack(values, axis=-1)

def basis_weights(steps_x, steps_y):
    coord_x = -1.0 + 2.0 * steps_x.astype(jnp.float32) / Q
    coord_y = -1.0 + 2.0 * steps_y.astype(jnp.float32) / Q
    along_x = lagrange(coord_x)
    along_y = lagrange(coord_y)
    weights = along_x[..., :, None] * along_y[..., None, :]
    return weights.reshape(steps_x.shape + (25,)).astype(jnp.bfloat16)

def dft_table():
    times = jnp.arange(T_SIZE, dtype=jnp.int32)[:, None]
    bins = jnp.arange(NF, dtype=jnp.int32)[None, :]
    phase = (times * bins % T_SIZE).astype(jnp.float32) * (2.0 * math.pi / T_SIZE)
    scale = 1.0 / math.sqrt(T_SIZE)
    return jnp.concatenate([jnp.cos(phase) * scale, -jnp.sin(phase) * scale], axis=1)

def transform(trace):
    table = dft_table()
    return jnp.dot(trace.astype(jnp.float32), table, precision=lax.Precision.HIGHEST).astype(jnp.bfloat16)

def reference(strain_db, owner, local_elem, lattice, pair_source, pair_receiver, filters):
    block = min(1024, CELLS)
    count = CELLS // block
    spectra_list = []
    for group in range(N_FRAME):
        db_group = strain_db[group]
        element = (owner[group, :, 0] * E_DEV + local_elem[group]).astype(jnp.int32)

        def one_block(items):
            elem_ids, steps_x, steps_y = items
            weights = basis_weights(steps_x, steps_y)
            picked = db_group[elem_ids]
            trace = jnp.einsum('bp,bpct->bct', weights.astype(jnp.float32), picked.astype(jnp.float32))
            return transform(trace.astype(jnp.bfloat16))
        spec = lax.map(one_block, (element.reshape(count, block), lattice[group, 0].reshape(count, block), lattice[group, 1].reshape(count, block)))
        spectra_list.append(spec.reshape(CELLS, C, 2 * NF))
    spectra = jnp.stack(spectra_list, axis=0)
    half_groups = N_FRAME // 2

    def pair_kernel(indices):
        source, receiver = indices
        first = spectra[source].astype(jnp.float32)
        second = spectra[receiver + half_groups].astype(jnp.float32)
        product = lax.optimization_barrier(jnp.sum(first * second, axis=1))
        cross = product[:, :NF] + product[:, NF:]
        return jnp.dot(filters, cross.T, precision=lax.Precision.HIGHEST) / math.sqrt(NF)
    return lax.map(pair_kernel, (pair_source, pair_receiver))
```

```python
import functools
import math

import jax
import jax.numpy as jnp
import ml_dtypes
import numpy as np
from jax import lax
from jax.experimental import pallas as pl
from jax.experimental.pallas import tpu as pltpu
from jax.sharding import PartitionSpec as P

C = 6
T = 256
NF = 64
Q = 64
NP = 25
E = 128
CELLS = 128
G = 8
NE = 16
DEV = G * NE
CAP = 12
PAIRS = 16
FILT = 64
ROWS = 24
WIDE = 384
UNROLL = 5
SPLIT = 2
BLOCK = 16
SLOTS = BLOCK * CAP
HALF = BLOCK // 2
ORDER = (0, 2, 4, 1, 3, 5)
MESH = pl.DeviceIdType.MESH

gll_nodes = [-1.0, -math.sqrt(3.0 / 7.0), 0.0, math.sqrt(3.0 / 7.0), 1.0]


def dft_table():
    phase = (np.arange(T)[:, None] * np.arange(NF)[None, :] % T) * (2.0 * math.pi / T)
    table = np.concatenate([np.cos(phase), -np.sin(phase)], axis=1) / math.sqrt(T)
    return table.astype(ml_dtypes.bfloat16)


def basis_rows():
    lane = lax.broadcasted_iota(jnp.int32, (1, 128), 1)
    rows = []
    for part in range(2):
        own = lane // 5 if part == 0 else lane % 5
        out = [jnp.zeros((1, 128), jnp.float32) for _ in range(5)]
        for i in range(5):
            others = [gll_nodes[m] for m in range(5) if m != i]
            scale = 1.0
            for node in others:
                scale *= gll_nodes[i] - node
            for k, value in enumerate(others + [1.0 / scale]):
                out[k] = jnp.where((own == i) & (lane < NP), value, out[k])
        rows += out
    return rows


def offset(block, dd):
    dy = (block + dd + dd // 4 + 1) % 4
    return (dd + 1) % 4, dy, (dd // 4 + 1) % 4, block // 4


SELF = 15
SELF_BLOCK = next(block for block in range(4) if offset(block, SELF) == (0, 0, 0, 0))


def slot_table():
    table = np.zeros((DEV // BLOCK, SLOTS, 128), np.float32)
    for block in range(DEV // BLOCK):
        for dd in range(BLOCK):
            dx, dy, dz, dc = offset(block, dd)
            for j in range(CAP):
                size = BLOCK if block else HALF
                part, at = divmod(dd, size)
                row = at * 8 + j if j < 8 else size * 8 + at * 4 + j - 8
                table[block, part * size * CAP + row, (dy * 2 + dc) * NE + dx * 4 + dz] = 1.0
    return table.astype(ml_dtypes.bfloat16)


def constants():
    return np.concatenate([dft_table(), slot_table().reshape(-1, 128)])


def iota(shape, dim):
    return lax.broadcasted_iota(jnp.int32, shape, dim)


def nt(a, b):
    return lax.dot_general(
        a, b, (((1,), (1,)), ((), ())), preferred_element_type=jnp.float32
    )


def nn(a, b):
    return jnp.dot(a, b, preferred_element_type=jnp.float32)


def kernel(
    db_hbm, owner_hbm, elem_hbm, lattice_hbm, source_hbm, receiver_hbm, filters_hbm, constants_hbm,
    out_hbm,
    owner_ref, elem_ref, lattice_ref, source_ref, receiver_ref, filters_ref, constants_ref,
    raw, db, asked, middle, wanted, dense_a, dense_b, send, recv, onehot, spectra, cross, result,
    small_sem, load_sem, ask_send, ask_recv, pass_send, pass_recv, ret_send, ret_recv, out_sem,
):
    me_f = lax.axis_index("frame")
    me_e = lax.axis_index("elem")
    me = me_f * NE + me_e
    me_x, me_z = lax.div(me_e, 4), lax.rem(me_e, 4)

    me_y, me_c = lax.div(me_f, 2), lax.rem(me_f, 2)

    def frame_at(dy, dc):
        return lax.rem(me_y + (dy + 4), 4) * 2 + lax.rem(me_c + dc, 2)

    def elem_at(dx, dz):
        return lax.rem(me_x + (dx + 4), 4) * 4 + lax.rem(me_z + (dz + 4), 4)

    small = [
        pltpu.make_async_copy(src, dst, small_sem.at[k])
        for k, (src, dst) in enumerate(
            (
                (owner_hbm, owner_ref),
                (elem_hbm, elem_ref),
                (lattice_hbm, lattice_ref),
                (constants_hbm, constants_ref),
                (filters_hbm, filters_ref),
                (source_hbm, source_ref),
                (receiver_hbm, receiver_ref),
            )
        )
    ]
    for copy in small[:4]:
        copy.start()

    barrier = pltpu.get_barrier_semaphore()
    for k in range(1, G):
        pl.semaphore_signal(
            barrier, inc=1, device_id=(frame_at(k // 2, k % 2), me_e), device_id_type=MESH
        )
    for k in range(1, NE):
        pl.semaphore_signal(
            barrier, inc=1, device_id=(me_f, elem_at(k // 4, k % 4)), device_id_type=MESH
        )

    def load(p):
        return [
            pltpu.make_async_copy(
                db_hbm.at[p, :, :, pl.ds(half * 128, 128)], raw.at[p, half], load_sem.at[p]
            )
            for half in range(2)
        ]

    def start_load(p, carry):
        for copy in load(p):
            copy.start()
        return carry

    lax.fori_loop(0, NP, start_load, 0)
    for copy in small[4:]:
        copy.start()
    for copy in small[:3]:
        copy.wait()

    owner = owner_ref[...]
    columns = jnp.transpose(owner.astype(jnp.float32)).astype(jnp.int32)
    lane = iota((CELLS, CELLS), 1)
    sub = iota((CELLS, CELLS), 0)
    row16 = iota((16, CELLS), 0)
    for g in range(G):
        row = owner[g : g + 1, :]
        col = columns[:, g : g + 1]
        same = row == col
        rank = jnp.sum(jnp.where(same & (sub < lane), 1, 0), axis=0, keepdims=True)
        hot_e = jnp.where(row16 == row, 1.0, 0.0).astype(jnp.bfloat16)
        here = row16 == rank
        parts = [
            jnp.where(here, value.astype(jnp.float32), 0.0)
            for value in (
                elem_ref[g : g + 1, :] + 1,
                lattice_ref[2 * g : 2 * g + 1, :],
                lattice_ref[2 * g + 1 : 2 * g + 2, :],
            )
        ]
        parts.append(jnp.zeros((CELLS - 48, CELLS), jnp.float32))
        values = jnp.concatenate(parts, axis=0).astype(jnp.bfloat16)
        asked[g] = nt(hot_e, values).reshape(NE, 1, 128)

    pl.semaphore_wait(barrier, G - 1 + NE - 1)
    for k in range(1, G):
        to_f = frame_at(-(k // 2), k % 2)
        pltpu.make_async_remote_copy(
            src_ref=asked.at[to_f],
            dst_ref=middle.at[k],
            send_sem=ask_send,
            recv_sem=ask_recv,
            device_id=(to_f, me_e),
            device_id_type=MESH,
        ).start()
    pltpu.make_async_copy(asked.at[me_f], middle.at[0], ask_recv).start()

    small[3].wait()
    table = constants_ref[:T]

    def to_spectrum(step, carry):
        for k in range(UNROLL):
            at = raw.at[step * UNROLL + k]
            pltpu.make_async_copy(at, at, load_sem.at[step * UNROLL + k]).wait()
        for k in range(UNROLL):
            p = step * UNROLL + k
            halves = [raw[p, half].reshape(C * E, 128) for half in range(2)]
            value = nn(jnp.concatenate(halves, axis=1), table).astype(jnp.bfloat16)
            at = pl.multiple_of(p * E, E)
            for k, c in enumerate(ORDER):
                db[k, pl.ds(at, E), :] = value[c * E : (c + 1) * E, :]
        return carry

    lax.fori_loop(0, SPLIT, to_spectrum, 0)
    pltpu.make_async_copy(middle, middle, ask_recv).wait()
    for k in range(1, NE):
        to_e = elem_at(-(k // 4), -(k % 4))
        pltpu.make_async_remote_copy(
            src_ref=middle.at[:, to_e],
            dst_ref=wanted.at[:, k],
            send_sem=pass_send,
            recv_sem=pass_recv,
            device_id=(me_f, to_e),
            device_id_type=MESH,
        ).start()
    pltpu.make_async_copy(middle.at[:, me_e], wanted.at[:, 0], pass_recv).start()
    lax.fori_loop(SPLIT, NP // UNROLL, to_spectrum, 0)
    for copy in small[4:]:
        copy.wait()
    pltpu.make_async_copy(wanted, wanted, pass_recv).wait()

    def own_slots(size):
        r = iota((size * CAP, 128), 0)
        j_row = jnp.where(r < size * 8, r & 7, 8 + (r & 3))
        return (iota((size * CAP, 128), 1) & 15) == j_row

    spread = jnp.where((iota((128, WIDE), 0) >> 4) == (iota((128, WIDE), 1) >> 7), 1.0, 0.0).astype(jnp.bfloat16)
    lane_f = (iota((1, 128), 1) + 1).astype(jnp.float32)

    basis = basis_rows()
    wanted_rows = wanted[...].reshape(DEV, 128).astype(jnp.bfloat16)

    def weigh(first, size, dense):
        rows = pl.ds(pl.multiple_of(T + first * CAP, 32), size * CAP)
        rows = nn(constants_ref[rows, :], wanted_rows)
        rows = jnp.where(own_slots(size), rows, 0.0).astype(jnp.bfloat16)
        wide = nn(rows, spread)
        hit = wide[:, :128] == lane_f
        weight = None
        for part in range(2):
            coord = wide[:, 128 * (part + 1) : 128 * (part + 2)] * (2.0 / Q) - 1.0
            value = basis[part * 5 + 4]
            for k in range(4):
                value = value * (coord - basis[part * 5 + k])
            weight = value if weight is None else weight * value
        for p in range(NP):
            dense[p, : size * CAP] = jnp.where(hit, weight[:, p : p + 1], 0.0).astype(jnp.bfloat16)

    def interpolate(first, size, dense):
        lhs = jnp.concatenate([dense[p, : size * CAP] for p in range(NP)], axis=1)
        rhs = jnp.concatenate([db[k] for k in range(C)], axis=1)
        result = nn(lhs, rhs)
        low = iota((8, 128), 0) < 4
        for dd in range(size):
            parts = []
            for q in range(3):
                even = result[:, q * 128 : (q + 1) * 128]
                odd = result[:, WIDE + q * 128 : WIDE + (q + 1) * 128]
                parts += [even[dd * 8 : (dd + 1) * 8], odd[dd * 8 : (dd + 1) * 8]]
                at = size * 8 + (dd // 2) * 8
                even, odd = even[at : at + 8], odd[at : at + 8]
                if dd % 2 == 0:
                    parts.append(jnp.where(low, even, pltpu.roll(odd, 4, 0)))
                else:
                    parts.append(jnp.where(low, pltpu.roll(even, 4, 0), odd))
            send[first + dd] = jnp.concatenate(parts, axis=0).astype(jnp.bfloat16)

    def give(b, dd):
        dx, _, dz, _ = offset(0, dd)
        dy, dc = lax.rem(b + (dd + dd // 4 + 1), 4), lax.div(b, 4)
        pltpu.make_async_remote_copy(
            src_ref=send.at[b * BLOCK + dd],
            dst_ref=recv.at[me],
            send_sem=ret_send,
            recv_sem=ret_recv.at[me_f],
            device_id=(frame_at(dy, dc), elem_at(dx, dz)),
            device_id_type=MESH,
        ).start()

    def give_block(b):
        for dd in range(BLOCK):
            if dd == SELF:

                @pl.when(b != SELF_BLOCK)
                def _():
                    give(b, SELF)
            else:
                give(b, dd)

    for part, dense in enumerate((dense_a, dense_b)):
        weigh(part * HALF, HALF, dense)
        interpolate(part * HALF, HALF, dense)
        for dd in range(part * HALF, (part + 1) * HALF):
            give(0, dd)

    def two_blocks(i, carry):
        b = 2 * i + 1
        weigh((b + 1) * BLOCK, BLOCK, dense_b)
        interpolate(b * BLOCK, BLOCK, dense_a)
        give_block(b)
        weigh((b + 2) * BLOCK, BLOCK, dense_a)
        interpolate((b + 1) * BLOCK, BLOCK, dense_b)
        give_block(b + 1)
        return carry

    last = DEV // BLOCK - 1
    weigh(BLOCK, BLOCK, dense_a)
    lax.fori_loop(0, last // 2, two_blocks, 0)
    interpolate(last * BLOCK, BLOCK, dense_a)
    for dd in range(BLOCK):
        give(last, dd)
    pltpu.make_async_copy(send.at[SELF_BLOCK * BLOCK + SELF], recv.at[me], ret_recv.at[me_f]).start()

    wide_lane = iota((CELLS, WIDE), 1)
    for g in range(G):
        row = owner[g : g + 1, :]
        col = columns[:, g : g + 1]
        rank = jnp.sum(jnp.where((row == col) & (lane < sub), 1.0, 0.0), axis=1, keepdims=True).astype(jnp.int32)
        at_even = col * ROWS + jnp.where(rank < 8, rank, rank + 8)
        at_odd = col * ROWS + jnp.where(rank < 8, rank + 8, rank + 12)
        onehot[g, :CELLS] = jnp.where(wide_lane == at_even, 1.0, 0.0).astype(jnp.bfloat16)
        onehot[g, CELLS:] = jnp.where(wide_lane == at_odd, 1.0, 0.0).astype(jnp.bfloat16)

    for dc in range(2):
        groups = [frame_at(dy, dc) for dy in range(4)]
        for g in groups:
            block = recv.at[pl.ds(g * NE, NE)]
            pltpu.make_async_copy(block, block, ret_recv.at[g]).wait()
        for g in groups:
            rows = recv[pl.ds(g * NE, NE)].astype(jnp.float32)
            rows = [rows[:, q * ROWS : (q + 1) * ROWS].reshape(NE * ROWS, 128) for q in range(3)]
            spectra[g] = nn(onehot[g], jnp.concatenate(rows, axis=1).astype(jnp.bfloat16))

    def products(i, carry):
        at = pl.multiple_of(i * 8, 8)
        total = [None] * 16
        for half in range(2):
            for k in range(3):
                pieces = [
                    spectra[g, pl.ds(at + half * CELLS, 8), k * 128 : (k + 1) * 128] for g in range(G)
                ]
                for s in range(4):
                    for q in range(4):
                        term = pieces[s] * pieces[4 + q]
                        n = s * 4 + q
                        total[n] = term if total[n] is None else total[n] + term
        for n in range(16):
            cross[n, pl.ds(at, 8), :] = total[n]
        return carry

    lax.fori_loop(0, CELLS // 8, products, 0)

    bank = filters_ref[...] * (1.0 / math.sqrt(NF))
    bank = jnp.concatenate([bank, bank], axis=1)
    bank_high = bank.astype(jnp.bfloat16)
    bank_low = (bank - bank_high.astype(jnp.float32)).astype(jnp.bfloat16)
    bank = jnp.concatenate([bank_high, bank_low], axis=0)
    bank = jnp.concatenate([bank, bank], axis=1)

    for p in range(PAIRS):
        value = cross[source_ref[p] * 4 + receiver_ref[p]]
        high = value.astype(jnp.bfloat16)
        low = (value - high.astype(jnp.float32)).astype(jnp.bfloat16)
        both = nt(bank, jnp.concatenate([high, low], axis=1))
        result[p] = both[:FILT] + both[FILT:]
        pltpu.make_async_copy(result.at[p], out_hbm.at[p], out_sem).start()

    pltpu.make_async_copy(result, out_hbm, out_sem).wait()
    others = pl.ds(0, G - 1)
    pltpu.make_async_copy(asked.at[others], asked.at[others], ask_send).wait()
    others = pl.ds(0, NE - 1)
    pltpu.make_async_copy(middle.at[:, others], middle.at[:, others], pass_send).wait()
    others = pl.ds(0, DEV - 1)
    pltpu.make_async_copy(send.at[others], send.at[others], ret_send).wait()


def local(strain_db, owner, local_elem, lattice, pair_source, pair_receiver, filters):
    hbm = pl.BlockSpec(memory_space=pltpu.HBM)
    database = jnp.transpose(strain_db[0], (1, 2, 0, 3))
    return pl.pallas_call(
        kernel,
        out_shape=jax.ShapeDtypeStruct((PAIRS, FILT, CELLS), jnp.float32),
        in_specs=[hbm] * 8,
        out_specs=hbm,
        scratch_shapes=[
            pltpu.VMEM((G, CELLS), jnp.int32),
            pltpu.VMEM((G, CELLS), jnp.int32),
            pltpu.VMEM((2 * G, CELLS), jnp.int32),
            pltpu.SMEM((PAIRS,), jnp.int32),
            pltpu.SMEM((PAIRS,), jnp.int32),
            pltpu.VMEM((FILT, NF), jnp.float32),
            pltpu.VMEM((T + DEV * CAP, 128), jnp.bfloat16),
            pltpu.VMEM((NP, 2, C, E, 128), jnp.bfloat16),
            pltpu.VMEM((C, NP * E, 128), jnp.bfloat16),
            pltpu.VMEM((G, NE, 1, 128), jnp.float32),
            pltpu.VMEM((G, NE, 1, 128), jnp.float32),
            pltpu.VMEM((G, NE, 1, 128), jnp.float32),
            pltpu.VMEM((NP, SLOTS, 128), jnp.bfloat16),
            pltpu.VMEM((NP, SLOTS, 128), jnp.bfloat16),
            pltpu.VMEM((DEV, 3 * ROWS, 128), jnp.bfloat16),
            pltpu.VMEM((DEV, 3 * ROWS, 128), jnp.bfloat16),
            pltpu.VMEM((G, 2 * CELLS, WIDE), jnp.bfloat16),
            pltpu.VMEM((G, 2 * CELLS, WIDE), jnp.float32),
            pltpu.VMEM((16, CELLS, 128), jnp.float32),
            pltpu.VMEM((PAIRS, FILT, CELLS), jnp.float32),
            pltpu.SemaphoreType.DMA((7,)),
            pltpu.SemaphoreType.DMA((NP,)),
            pltpu.SemaphoreType.DMA,
            pltpu.SemaphoreType.DMA,
            pltpu.SemaphoreType.DMA,
            pltpu.SemaphoreType.DMA,
            pltpu.SemaphoreType.DMA,
            pltpu.SemaphoreType.DMA((G,)),
            pltpu.SemaphoreType.DMA,
        ],
        compiler_params=pltpu.CompilerParams(
            collective_id=0, has_side_effects=True, vmem_limit_bytes=60 * 2**20
        ),
    )(
        database,
        owner.reshape(G, CELLS),
        local_elem,
        lattice.reshape(2 * G, CELLS),
        pair_source,
        pair_receiver,
        filters,
        jnp.asarray(constants()),
    )


def solution(mesh):
    placed = (
        P("frame", "elem", None, None, None),
        P(None, ("frame", "elem"), None),
        P(None, ("frame", "elem")),
        P(None, None, ("frame", "elem")),
        P(),
        P(),
        P(),
    )
    return jax.shard_map(
        local,
        mesh=mesh,
        in_specs=placed,
        out_specs=P(None, None, ("frame", "elem")),
        check_vma=False,
    )
```

```python
import functools
import math

import jax
import jax.numpy as jnp
import ml_dtypes
import numpy as np
from jax import lax
from jax.experimental import pallas as pl
from jax.experimental.pallas import tpu as pltpu
from jax.sharding import PartitionSpec as P

C = 6
T = 256
NF = 64
Q = 64
NP = 25
E = 128
CELLS = 128
G = 8
NE = 16
DEV = G * NE
CAP = 12
PAIRS = 16
FILT = 64
ROWS = 24
WIDE = 384
UNROLL = 5
SPLIT = 2
BLOCK = 16
SLOTS = BLOCK * CAP
EARLY = 2
HALF = BLOCK // 2
ORDER = (0, 2, 4, 1, 3, 5)
MESH = pl.DeviceIdType.MESH

gll_nodes = [-1.0, -math.sqrt(3.0 / 7.0), 0.0, math.sqrt(3.0 / 7.0), 1.0]


def dft_table():
    phase = (np.arange(T)[:, None] * np.arange(NF)[None, :] % T) * (2.0 * math.pi / T)
    table = np.concatenate([np.cos(phase), -np.sin(phase)], axis=1) / math.sqrt(T)
    return table.astype(ml_dtypes.bfloat16)


def basis_rows():
    lane = lax.broadcasted_iota(jnp.int32, (1, 128), 1)
    rows = []
    for part in range(2):
        own = lane // 5 if part == 0 else lane % 5
        out = [jnp.zeros((1, 128), jnp.float32) for _ in range(5)]
        for i in range(5):
            others = [gll_nodes[m] for m in range(5) if m != i]
            scale = 1.0
            for node in others:
                scale *= gll_nodes[i] - node
            for k, value in enumerate(others + [1.0 / scale]):
                out[k] = jnp.where((own == i) & (lane < NP), value, out[k])
        rows += out
    return rows


def offset(block, dd):
    dy = (block + dd + dd // 4 + 1) % 4
    return (dd + 1) % 4, dy, (dd // 4 + 1) % 4, block // 4


SELF = 15
SELF_BLOCK = next(block for block in range(4) if offset(block, SELF) == (0, 0, 0, 0))


def slot_table():
    table = np.zeros((DEV // BLOCK, SLOTS, 128), np.float32)
    for block in range(DEV // BLOCK):
        for dd in range(BLOCK):
            dx, dy, dz, dc = offset(block, dd)
            for j in range(CAP):
                size = BLOCK if block >= EARLY else HALF
                part, at = divmod(dd, size)
                row = at * 8 + j if j < 8 else size * 8 + at * 4 + j - 8
                table[block, part * size * CAP + row, (dy * 2 + dc) * NE + dx * 4 + dz] = 1.0
    return table.astype(ml_dtypes.bfloat16)


def constants():
    return np.concatenate([dft_table(), slot_table().reshape(-1, 128)])


def iota(shape, dim):
    return lax.broadcasted_iota(jnp.int32, shape, dim)


def nt(a, b):
    return lax.dot_general(
        a, b, (((1,), (1,)), ((), ())), preferred_element_type=jnp.float32
    )


def nn(a, b):
    return jnp.dot(a, b, preferred_element_type=jnp.float32)


def kernel(
    db_hbm, owner_hbm, elem_hbm, lattice_hbm, source_hbm, receiver_hbm, filters_hbm, constants_hbm,
    out_hbm, staged,
    owner_ref, elem_ref, lattice_ref, source_ref, receiver_ref, filters_ref, constants_ref,
    raw, db, asked, middle, wanted, dense_a, dense_b, dense_c, send, recv, onehot, spectra, cross, result,
    small_sem, load_sem, ask_send, ask_recv, pass_send, pass_recv, ret_send, ret_recv, out_sem, stage_sem,
):
    me_f = lax.axis_index("frame")
    me_e = lax.axis_index("elem")
    me = me_f * NE + me_e
    me_x, me_z = lax.div(me_e, 4), lax.rem(me_e, 4)

    me_y, me_c = lax.div(me_f, 2), lax.rem(me_f, 2)

    def frame_at(dy, dc):
        return lax.rem(me_y + (dy + 4), 4) * 2 + lax.rem(me_c + dc, 2)

    def elem_at(dx, dz):
        return lax.rem(me_x + (dx + 4), 4) * 4 + lax.rem(me_z + (dz + 4), 4)

    small = [
        pltpu.make_async_copy(src, dst, small_sem.at[k])
        for k, (src, dst) in enumerate(
            (
                (owner_hbm, owner_ref),
                (elem_hbm, elem_ref),
                (lattice_hbm, lattice_ref),
                (constants_hbm, constants_ref),
                (filters_hbm, filters_ref),
                (source_hbm, source_ref),
                (receiver_hbm, receiver_ref),
            )
        )
    ]
    for copy in small[:4]:
        copy.start()

    barrier = pltpu.get_barrier_semaphore()
    for k in range(1, G):
        pl.semaphore_signal(
            barrier, inc=1, device_id=(frame_at(k // 2, k % 2), me_e), device_id_type=MESH
        )
    for k in range(1, NE):
        pl.semaphore_signal(
            barrier, inc=1, device_id=(me_f, elem_at(k // 4, k % 4)), device_id_type=MESH
        )

    def load(p):
        return [
            pltpu.make_async_copy(
                db_hbm.at[p, :, :, pl.ds(half * 128, 128)], raw.at[p, half], load_sem.at[p]
            )
            for half in range(2)
        ]

    def start_load(p, carry):
        for copy in load(p):
            copy.start()
        return carry

    lax.fori_loop(0, NP, start_load, 0)
    for copy in small[4:]:
        copy.start()
    for copy in small[:3]:
        copy.wait()

    owner = owner_ref[...]
    columns = jnp.transpose(owner.astype(jnp.float32)).astype(jnp.int32)
    lane = iota((CELLS, CELLS), 1)
    sub = iota((CELLS, CELLS), 0)
    row16 = iota((16, CELLS), 0)
    for g in range(G):
        row = owner[g : g + 1, :]
        col = columns[:, g : g + 1]
        same = row == col
        rank = jnp.sum(jnp.where(same & (sub < lane), 1, 0), axis=0, keepdims=True)
        hot_e = jnp.where(row16 == row, 1.0, 0.0).astype(jnp.bfloat16)
        here = row16 == rank
        parts = [
            jnp.where(here, value.astype(jnp.float32), 0.0)
            for value in (
                elem_ref[g : g + 1, :] + 1,
                lattice_ref[2 * g : 2 * g + 1, :],
                lattice_ref[2 * g + 1 : 2 * g + 2, :],
            )
        ]
        parts.append(jnp.zeros((CELLS - 48, CELLS), jnp.float32))
        values = jnp.concatenate(parts, axis=0).astype(jnp.bfloat16)
        asked[g] = nt(hot_e, values).reshape(NE, 1, 128)

    pl.semaphore_wait(barrier, G - 1 + NE - 1)
    for k in range(1, G):
        to_f = frame_at(-(k // 2), k % 2)
        pltpu.make_async_remote_copy(
            src_ref=asked.at[to_f],
            dst_ref=middle.at[k],
            send_sem=ask_send,
            recv_sem=ask_recv,
            device_id=(to_f, me_e),
            device_id_type=MESH,
        ).start()
    pltpu.make_async_copy(asked.at[me_f], middle.at[0], ask_recv).start()

    small[3].wait()
    table = constants_ref[:T]

    def to_spectrum(step, carry):
        for k in range(UNROLL):
            at = raw.at[step * UNROLL + k]
            pltpu.make_async_copy(at, at, load_sem.at[step * UNROLL + k]).wait()
        for k in range(UNROLL):
            p = step * UNROLL + k
            halves = [raw[p, half].reshape(C * E, 128) for half in range(2)]
            value = nn(jnp.concatenate(halves, axis=1), table).astype(jnp.bfloat16)
            at = pl.multiple_of(p * E, E)
            for k, c in enumerate(ORDER):
                db[k, pl.ds(at, E), :] = value[c * E : (c + 1) * E, :]
        return carry

    lax.fori_loop(0, SPLIT, to_spectrum, 0)
    pltpu.make_async_copy(middle, middle, ask_recv).wait()
    for k in range(1, NE):
        to_e = elem_at(-(k // 4), -(k % 4))
        pltpu.make_async_remote_copy(
            src_ref=middle.at[:, to_e],
            dst_ref=wanted.at[:, k],
            send_sem=pass_send,
            recv_sem=pass_recv,
            device_id=(me_f, to_e),
            device_id_type=MESH,
        ).start()
    pltpu.make_async_copy(middle.at[:, me_e], wanted.at[:, 0], pass_recv).start()
    lax.fori_loop(SPLIT, NP // UNROLL, to_spectrum, 0)
    for copy in small[4:]:
        copy.wait()
    pltpu.make_async_copy(wanted, wanted, pass_recv).wait()

    def own_slots(size):
        r = iota((size * CAP, 128), 0)
        j_row = jnp.where(r < size * 8, r & 7, 8 + (r & 3))
        return (iota((size * CAP, 128), 1) & 15) == j_row

    spread = jnp.where((iota((128, WIDE), 0) >> 4) == (iota((128, WIDE), 1) >> 7), 1.0, 0.0).astype(jnp.bfloat16)
    lane_f = (iota((1, 128), 1) + 1).astype(jnp.float32)

    basis = basis_rows()
    wanted_rows = wanted[...].reshape(DEV, 128).astype(jnp.bfloat16)

    def weigh(first, size, dense):
        rows = pl.ds(pl.multiple_of(T + first * CAP, 32), size * CAP)
        rows = nn(constants_ref[rows, :], wanted_rows)
        rows = jnp.where(own_slots(size), rows, 0.0).astype(jnp.bfloat16)
        wide = nn(rows, spread)
        hit = wide[:, :128] == lane_f
        weight = None
        for part in range(2):
            coord = wide[:, 128 * (part + 1) : 128 * (part + 2)] * (2.0 / Q) - 1.0
            value = basis[part * 5 + 4]
            for k in range(4):
                value = value * (coord - basis[part * 5 + k])
            weight = value if weight is None else weight * value
        for p in range(NP):
            dense[p, : size * CAP] = jnp.where(hit, weight[:, p : p + 1], 0.0).astype(jnp.bfloat16)

    def interpolate(first, size, dense):
        lhs = jnp.concatenate([dense[p, : size * CAP] for p in range(NP)], axis=1)
        rhs = jnp.concatenate([db[k] for k in range(C)], axis=1)
        result = nn(lhs, rhs)
        low = iota((8, 128), 0) < 4
        for dd in range(size):
            parts = []
            for q in range(3):
                even = result[:, q * 128 : (q + 1) * 128]
                odd = result[:, WIDE + q * 128 : WIDE + (q + 1) * 128]
                parts += [even[dd * 8 : (dd + 1) * 8], odd[dd * 8 : (dd + 1) * 8]]
                at = size * 8 + (dd // 2) * 8
                even, odd = even[at : at + 8], odd[at : at + 8]
                if dd % 2 == 0:
                    parts.append(jnp.where(low, even, pltpu.roll(odd, 4, 0)))
                else:
                    parts.append(jnp.where(low, pltpu.roll(even, 4, 0), odd))
            send[first + dd] = jnp.concatenate(parts, axis=0).astype(jnp.bfloat16)

    def give(b, dd, source=send):
        dx, _, dz, _ = offset(0, dd)
        dy, dc = lax.rem(b + (dd + dd // 4 + 1), 4), lax.div(b, 4)
        pltpu.make_async_remote_copy(
            src_ref=source.at[b * BLOCK + dd],
            dst_ref=recv.at[me],
            send_sem=ret_send,
            recv_sem=ret_recv.at[me_f],
            device_id=(frame_at(dy, dc), elem_at(dx, dz)),
            device_id_type=MESH,
        ).start()

    parts = EARLY * BLOCK // HALF
    for part in range(parts):
        dense = dense_a if part % 2 == 0 else dense_b
        weigh(part * HALF, HALF, dense)
        if part == parts - 1:
            weigh(EARLY * BLOCK, BLOCK, dense_c)
        interpolate(part * HALF, HALF, dense)
        for index in range(part * HALF, (part + 1) * HALF):
            if index != SELF_BLOCK * BLOCK + SELF:
                give(index // BLOCK, index % BLOCK)

    def staging(b):
        second = pl.ds(b * BLOCK + HALF, HALF)
        return pltpu.make_async_copy(send.at[second], staged.at[second], stage_sem.at[b])

    def give_direct(b):
        staging(b).start()
        for dd in range(HALF):
            give(b, dd)

    def give_staged(b):
        staging(b).wait()
        for dd in range(HALF, BLOCK):
            give(b, dd, staged)

    def two_blocks(i, carry):
        b = 2 * i + EARLY
        weigh((b + 1) * BLOCK, BLOCK, dense_a)
        interpolate(b * BLOCK, BLOCK, dense_c)
        give_direct(b)

        @pl.when(i > 0)
        def _():
            give_staged(b - 1)

        weigh(jnp.minimum(b + 2, DEV // BLOCK - 1) * BLOCK, BLOCK, dense_c)
        interpolate((b + 1) * BLOCK, BLOCK, dense_a)
        give_direct(b + 1)
        give_staged(b)
        return carry

    lax.fori_loop(0, (DEV // BLOCK - EARLY) // 2, two_blocks, 0)
    give_staged(DEV // BLOCK - 1)
    pltpu.make_async_copy(send.at[SELF_BLOCK * BLOCK + SELF], recv.at[me], ret_recv.at[me_f]).start()

    wide_lane = iota((CELLS, WIDE), 1)
    for g in range(G):
        row = owner[g : g + 1, :]
        col = columns[:, g : g + 1]
        rank = jnp.sum(jnp.where((row == col) & (lane < sub), 1.0, 0.0), axis=1, keepdims=True).astype(jnp.int32)
        at_even = col * ROWS + jnp.where(rank < 8, rank, rank + 8)
        at_odd = col * ROWS + jnp.where(rank < 8, rank + 8, rank + 12)
        onehot[g, :CELLS] = jnp.where(wide_lane == at_even, 1.0, 0.0).astype(jnp.bfloat16)
        onehot[g, CELLS:] = jnp.where(wide_lane == at_odd, 1.0, 0.0).astype(jnp.bfloat16)

    for dc in range(2):
        groups = [frame_at(dy, dc) for dy in range(4)]
        for g in groups:
            block = recv.at[pl.ds(g * NE, NE)]
            pltpu.make_async_copy(block, block, ret_recv.at[g]).wait()
        for g in groups:
            rows = recv[pl.ds(g * NE, NE)].astype(jnp.float32)
            rows = [rows[:, q * ROWS : (q + 1) * ROWS].reshape(NE * ROWS, 128) for q in range(3)]
            spectra[g] = nn(onehot[g], jnp.concatenate(rows, axis=1).astype(jnp.bfloat16))

    def products(i, carry):
        at = pl.multiple_of(i * 8, 8)
        total = [None] * 16
        for half in range(2):
            for k in range(3):
                pieces = [
                    spectra[g, pl.ds(at + half * CELLS, 8), k * 128 : (k + 1) * 128] for g in range(G)
                ]
                for s in range(4):
                    for q in range(4):
                        term = pieces[s] * pieces[4 + q]
                        n = s * 4 + q
                        total[n] = term if total[n] is None else total[n] + term
        for n in range(16):
            cross[n, pl.ds(at, 8), :] = total[n]
        return carry

    lax.fori_loop(0, CELLS // 8, products, 0)

    bank = filters_ref[...] * (1.0 / math.sqrt(NF))
    bank = jnp.concatenate([bank, bank], axis=1)
    bank_high = bank.astype(jnp.bfloat16)
    bank_low = (bank - bank_high.astype(jnp.float32)).astype(jnp.bfloat16)
    bank = jnp.concatenate([bank_high, bank_low], axis=0)
    bank = jnp.concatenate([bank, bank], axis=1)

    for p in range(PAIRS):
        value = cross[source_ref[p] * 4 + receiver_ref[p]]
        high = value.astype(jnp.bfloat16)
        low = (value - high.astype(jnp.float32)).astype(jnp.bfloat16)
        both = nt(bank, jnp.concatenate([high, low], axis=1))
        result[p] = both[:FILT] + both[FILT:]
        pltpu.make_async_copy(result.at[p], out_hbm.at[p], out_sem).start()

    pltpu.make_async_copy(result, out_hbm, out_sem).wait()
    others = pl.ds(0, G - 1)
    pltpu.make_async_copy(asked.at[others], asked.at[others], ask_send).wait()
    others = pl.ds(0, NE - 1)
    pltpu.make_async_copy(middle.at[:, others], middle.at[:, others], pass_send).wait()
    others = pl.ds(0, DEV - 1)
    pltpu.make_async_copy(send.at[others], send.at[others], ret_send).wait()


def local(strain_db, owner, local_elem, lattice, pair_source, pair_receiver, filters):
    hbm = pl.BlockSpec(memory_space=pltpu.HBM)
    database = jnp.transpose(strain_db[0], (1, 2, 0, 3))
    result, _ = pl.pallas_call(
        kernel,
        out_shape=[
            jax.ShapeDtypeStruct((PAIRS, FILT, CELLS), jnp.float32),
            jax.ShapeDtypeStruct((DEV, 3 * ROWS, 128), jnp.bfloat16),
        ],
        in_specs=[hbm] * 8,
        out_specs=[hbm, hbm],
        scratch_shapes=[
            pltpu.VMEM((G, CELLS), jnp.int32),
            pltpu.VMEM((G, CELLS), jnp.int32),
            pltpu.VMEM((2 * G, CELLS), jnp.int32),
            pltpu.SMEM((PAIRS,), jnp.int32),
            pltpu.SMEM((PAIRS,), jnp.int32),
            pltpu.VMEM((FILT, NF), jnp.float32),
            pltpu.VMEM((T + DEV * CAP, 128), jnp.bfloat16),
            pltpu.VMEM((NP, 2, C, E, 128), jnp.bfloat16),
            pltpu.VMEM((C, NP * E, 128), jnp.bfloat16),
            pltpu.VMEM((G, NE, 1, 128), jnp.float32),
            pltpu.VMEM((G, NE, 1, 128), jnp.float32),
            pltpu.VMEM((G, NE, 1, 128), jnp.float32),
            pltpu.VMEM((NP, SLOTS, 128), jnp.bfloat16),
            pltpu.VMEM((NP, HALF * CAP, 128), jnp.bfloat16),
            pltpu.VMEM((NP, SLOTS, 128), jnp.bfloat16),
            pltpu.VMEM((DEV, 3 * ROWS, 128), jnp.bfloat16),
            pltpu.VMEM((DEV, 3 * ROWS, 128), jnp.bfloat16),
            pltpu.VMEM((G, 2 * CELLS, WIDE), jnp.bfloat16),
            pltpu.VMEM((G, 2 * CELLS, WIDE), jnp.float32),
            pltpu.VMEM((16, CELLS, 128), jnp.float32),
            pltpu.VMEM((PAIRS, FILT, CELLS), jnp.float32),
            pltpu.SemaphoreType.DMA((7,)),
            pltpu.SemaphoreType.DMA((NP,)),
            pltpu.SemaphoreType.DMA,
            pltpu.SemaphoreType.DMA,
            pltpu.SemaphoreType.DMA,
            pltpu.SemaphoreType.DMA,
            pltpu.SemaphoreType.DMA,
            pltpu.SemaphoreType.DMA((G,)),
            pltpu.SemaphoreType.DMA,
            pltpu.SemaphoreType.DMA((DEV // BLOCK,)),
        ],
        compiler_params=pltpu.CompilerParams(
            collective_id=0, has_side_effects=True, vmem_limit_bytes=60 * 2**20
        ),
    )(
        database,
        owner.reshape(G, CELLS),
        local_elem,
        lattice.reshape(2 * G, CELLS),
        pair_source,
        pair_receiver,
        filters,
        jnp.asarray(constants()),
    )
    return result


def solution(mesh):
    placed = (
        P("frame", "elem", None, None, None),
        P(None, ("frame", "elem"), None),
        P(None, ("frame", "elem")),
        P(None, None, ("frame", "elem")),
        P(),
        P(),
        P(),
    )
    return jax.shard_map(
        local,
        mesh=mesh,
        in_specs=placed,
        out_specs=P(None, None, ("frame", "elem")),
        check_vma=False,
    )
```

```python
import functools
import math

import jax
import jax.numpy as jnp
import ml_dtypes
import numpy as np
from jax import lax
from jax.experimental import pallas as pl
from jax.experimental.pallas import tpu as pltpu
from jax.sharding import PartitionSpec as P

C = 6
T = 256
NF = 64
Q = 64
NP = 25
E = 128
CELLS = 128
G = 8
NE = 16
DEV = G * NE
CAP = 12
PAIRS = 16
FILT = 64
ROWS = 24
WIDE = 384
UNROLL = 5
SPLIT = 2
BLOCK = 16
SLOTS = BLOCK * CAP
EARLY = 2
HALF = BLOCK // 2
ORDER = (0, 2, 4, 1, 3, 5)
MESH = pl.DeviceIdType.MESH

gll_nodes = [-1.0, -math.sqrt(3.0 / 7.0), 0.0, math.sqrt(3.0 / 7.0), 1.0]


def dft_table():
    phase = (np.arange(T)[:, None] * np.arange(NF)[None, :] % T) * (2.0 * math.pi / T)
    table = np.concatenate([np.cos(phase), -np.sin(phase)], axis=1) / math.sqrt(T)
    return table.astype(ml_dtypes.bfloat16)


def basis_rows():
    lane = lax.broadcasted_iota(jnp.int32, (1, 128), 1)
    rows = []
    for part in range(2):
        own = lane // 5 if part == 0 else lane % 5
        out = [jnp.zeros((1, 128), jnp.float32) for _ in range(5)]
        for i in range(5):
            others = [gll_nodes[m] for m in range(5) if m != i]
            scale = 1.0
            for node in others:
                scale *= gll_nodes[i] - node
            for k, value in enumerate(others + [1.0 / scale]):
                out[k] = jnp.where((own == i) & (lane < NP), value, out[k])
        rows += out
    return rows


def offset(block, dd):
    dy = (block + dd + dd // 4 + 1) % 4
    return (dd + 1) % 4, dy, (dd // 4 + 1) % 4, block // 4


SELF = 15
SELF_BLOCK = next(block for block in range(4) if offset(block, SELF) == (0, 0, 0, 0))


def slot_table():
    table = np.zeros((DEV // BLOCK, SLOTS, 128), np.float32)
    for block in range(DEV // BLOCK):
        for dd in range(BLOCK):
            dx, dy, dz, dc = offset(block, dd)
            for j in range(CAP):
                size = BLOCK if block >= EARLY else HALF
                part, at = divmod(dd, size)
                row = at * 8 + j if j < 8 else size * 8 + at * 4 + j - 8
                table[block, part * size * CAP + row, (dy * 2 + dc) * NE + dx * 4 + dz] = 1.0
    return table.astype(ml_dtypes.bfloat16)


def constants():
    return np.concatenate([dft_table(), slot_table().reshape(-1, 128)])


def iota(shape, dim):
    return lax.broadcasted_iota(jnp.int32, shape, dim)


def nt(a, b):
    return lax.dot_general(
        a, b, (((1,), (1,)), ((), ())), preferred_element_type=jnp.float32
    )


def nn(a, b):
    return jnp.dot(a, b, preferred_element_type=jnp.float32)


def kernel(
    db_hbm, owner_hbm, elem_hbm, lattice_hbm, source_hbm, receiver_hbm, filters_hbm, constants_hbm,
    out_hbm,
    owner_ref, elem_ref, lattice_ref, source_ref, receiver_ref, filters_ref, constants_ref,
    raw, db, asked, middle, wanted, dense_a, dense_b, dense_c, send, recv, onehot, spectra, cross, result,
    small_sem, load_sem, ask_send, ask_recv, pass_send, pass_recv, ret_send, ret_recv, out_sem,
):
    me_f = lax.axis_index("frame")
    me_e = lax.axis_index("elem")
    me = me_f * NE + me_e
    me_x, me_z = lax.div(me_e, 4), lax.rem(me_e, 4)

    me_y, me_c = lax.div(me_f, 2), lax.rem(me_f, 2)

    def frame_at(dy, dc):
        return lax.rem(me_y + (dy + 4), 4) * 2 + lax.rem(me_c + dc, 2)

    def elem_at(dx, dz):
        return lax.rem(me_x + (dx + 4), 4) * 4 + lax.rem(me_z + (dz + 4), 4)

    small = [
        pltpu.make_async_copy(src, dst, small_sem.at[k])
        for k, (src, dst) in enumerate(
            (
                (owner_hbm, owner_ref),
                (elem_hbm, elem_ref),
                (lattice_hbm, lattice_ref),
                (constants_hbm, constants_ref),
                (filters_hbm, filters_ref),
                (source_hbm, source_ref),
                (receiver_hbm, receiver_ref),
            )
        )
    ]
    for copy in small[:4]:
        copy.start()

    barrier = pltpu.get_barrier_semaphore()
    for k in range(1, G):
        pl.semaphore_signal(
            barrier, inc=1, device_id=(frame_at(k // 2, k % 2), me_e), device_id_type=MESH
        )
    for k in range(1, NE):
        pl.semaphore_signal(
            barrier, inc=1, device_id=(me_f, elem_at(k // 4, k % 4)), device_id_type=MESH
        )

    for step in range(NP // UNROLL):
        points = pl.ds(step * UNROLL, UNROLL)
        for half in range(2):
            pltpu.make_async_copy(
                db_hbm.at[points, :, :, pl.ds(half * 128, 128)], raw.at[points, half], load_sem.at[step]
            ).start()
    for copy in small[4:]:
        copy.start()
    for copy in small[:3]:
        copy.wait()

    owner = owner_ref[...]
    columns = jnp.transpose(owner.astype(jnp.float32)).astype(jnp.int32)
    lane = iota((CELLS, CELLS), 1)
    sub = iota((CELLS, CELLS), 0)
    row16 = iota((16, CELLS), 0)
    for g in range(G):
        row = owner[g : g + 1, :]
        col = columns[:, g : g + 1]
        same = row == col
        rank = jnp.sum(jnp.where(same & (sub < lane), 1, 0), axis=0, keepdims=True)
        hot_e = jnp.where(row16 == row, 1.0, 0.0).astype(jnp.bfloat16)
        here = row16 == rank
        parts = [
            jnp.where(here, value.astype(jnp.float32), 0.0)
            for value in (
                elem_ref[g : g + 1, :] + 1,
                lattice_ref[2 * g : 2 * g + 1, :],
                lattice_ref[2 * g + 1 : 2 * g + 2, :],
            )
        ]
        parts.append(jnp.zeros((CELLS - 48, CELLS), jnp.float32))
        values = jnp.concatenate(parts, axis=0).astype(jnp.bfloat16)
        asked[g] = nt(hot_e, values).reshape(NE, 1, 128)

    pl.semaphore_wait(barrier, G - 1 + NE - 1)
    for k in range(1, G):
        to_f = frame_at(-(k // 2), k % 2)
        pltpu.make_async_remote_copy(
            src_ref=asked.at[to_f],
            dst_ref=middle.at[k],
            send_sem=ask_send,
            recv_sem=ask_recv,
            device_id=(to_f, me_e),
            device_id_type=MESH,
        ).start()
    pltpu.make_async_copy(asked.at[me_f], middle.at[0], ask_recv).start()

    small[3].wait()
    table = constants_ref[:T]

    def to_spectrum(step, carry):
        points = raw.at[pl.ds(step * UNROLL, UNROLL)]
        pltpu.make_async_copy(points, points, load_sem.at[step]).wait()
        for k in range(UNROLL):
            p = step * UNROLL + k
            halves = [raw[p, half].reshape(C * E, 128) for half in range(2)]
            value = nn(jnp.concatenate(halves, axis=1), table).astype(jnp.bfloat16)
            at = pl.multiple_of(p * E, E)
            for k, c in enumerate(ORDER):
                db[k, pl.ds(at, E), :] = value[c * E : (c + 1) * E, :]
        return carry

    lax.fori_loop(0, SPLIT, to_spectrum, 0)
    pltpu.make_async_copy(middle, middle, ask_recv).wait()
    for k in range(1, NE):
        to_e = elem_at(-(k // 4), -(k % 4))
        pltpu.make_async_remote_copy(
            src_ref=middle.at[:, to_e],
            dst_ref=wanted.at[:, k],
            send_sem=pass_send,
            recv_sem=pass_recv,
            device_id=(me_f, to_e),
            device_id_type=MESH,
        ).start()
    pltpu.make_async_copy(middle.at[:, me_e], wanted.at[:, 0], pass_recv).start()
    lax.fori_loop(SPLIT, NP // UNROLL, to_spectrum, 0)
    for copy in small[4:]:
        copy.wait()
    pltpu.make_async_copy(wanted, wanted, pass_recv).wait()

    def own_slots(size):
        r = iota((size * CAP, 128), 0)
        j_row = jnp.where(r < size * 8, r & 7, 8 + (r & 3))
        return (iota((size * CAP, 128), 1) & 15) == j_row

    spread = jnp.where((iota((128, WIDE), 0) >> 4) == (iota((128, WIDE), 1) >> 7), 1.0, 0.0).astype(jnp.bfloat16)
    lane_f = (iota((1, 128), 1) + 1).astype(jnp.float32)

    basis = basis_rows()
    wanted_rows = wanted[...].reshape(DEV, 128).astype(jnp.bfloat16)

    def weigh(first, size, dense):
        rows = pl.ds(pl.multiple_of(T + first * CAP, 32), size * CAP)
        rows = nn(constants_ref[rows, :], wanted_rows)
        rows = jnp.where(own_slots(size), rows, 0.0).astype(jnp.bfloat16)
        wide = nn(rows, spread)
        hit = wide[:, :128] == lane_f
        weight = None
        for part in range(2):
            coord = wide[:, 128 * (part + 1) : 128 * (part + 2)] * (2.0 / Q) - 1.0
            value = basis[part * 5 + 4]
            for k in range(4):
                value = value * (coord - basis[part * 5 + k])
            weight = value if weight is None else weight * value
        for p in range(NP):
            dense[p, : size * CAP] = jnp.where(hit, weight[:, p : p + 1], 0.0).astype(jnp.bfloat16)

    def interpolate(first, size, dense):
        lhs = jnp.concatenate([dense[p, : size * CAP] for p in range(NP)], axis=1)
        rhs = jnp.concatenate([db[k] for k in range(C)], axis=1)
        result = nn(lhs, rhs)
        low = iota((8, 128), 0) < 4
        for dd in range(size):
            parts = []
            for q in range(3):
                even = result[:, q * 128 : (q + 1) * 128]
                odd = result[:, WIDE + q * 128 : WIDE + (q + 1) * 128]
                parts += [even[dd * 8 : (dd + 1) * 8], odd[dd * 8 : (dd + 1) * 8]]
                at = size * 8 + (dd // 2) * 8
                even, odd = even[at : at + 8], odd[at : at + 8]
                if dd % 2 == 0:
                    parts.append(jnp.where(low, even, pltpu.roll(odd, 4, 0)))
                else:
                    parts.append(jnp.where(low, pltpu.roll(even, 4, 0), odd))
            send[first + dd] = jnp.concatenate(parts, axis=0).astype(jnp.bfloat16)

    def give(b, dd):
        dx, _, dz, _ = offset(0, dd)
        dy, dc = lax.rem(b + (dd + dd // 4 + 1), 4), lax.div(b, 4)
        pltpu.make_async_remote_copy(
            src_ref=send.at[b * BLOCK + dd],
            dst_ref=recv.at[me],
            send_sem=ret_send,
            recv_sem=ret_recv.at[me_f],
            device_id=(frame_at(dy, dc), elem_at(dx, dz)),
            device_id_type=MESH,
        ).start()

    parts = EARLY * BLOCK // HALF
    for part in range(parts):
        dense = dense_a if part % 2 == 0 else dense_b
        weigh(part * HALF, HALF, dense)
        if part == parts - 1:
            weigh(EARLY * BLOCK, BLOCK, dense_c)
        interpolate(part * HALF, HALF, dense)
        for index in range(part * HALF, (part + 1) * HALF):
            if index != SELF_BLOCK * BLOCK + SELF:
                give(index // BLOCK, index % BLOCK)

    def two_blocks(i, carry):
        b = 2 * i + EARLY
        weigh((b + 1) * BLOCK, BLOCK, dense_a)
        interpolate(b * BLOCK, BLOCK, dense_c)
        for dd in range(BLOCK):
            give(b, dd)
        weigh(jnp.minimum(b + 2, DEV // BLOCK - 1) * BLOCK, BLOCK, dense_c)
        interpolate((b + 1) * BLOCK, BLOCK, dense_a)
        for dd in range(BLOCK):
            give(b + 1, dd)
        return carry

    lax.fori_loop(0, (DEV // BLOCK - EARLY) // 2, two_blocks, 0)
    pltpu.make_async_copy(send.at[SELF_BLOCK * BLOCK + SELF], recv.at[me], ret_recv.at[me_f]).start()

    wide_lane = iota((CELLS, WIDE), 1)
    for g in range(G):
        row = owner[g : g + 1, :]
        col = columns[:, g : g + 1]
        rank = jnp.sum(jnp.where((row == col) & (lane < sub), 1.0, 0.0), axis=1, keepdims=True).astype(jnp.int32)
        at_even = col * ROWS + jnp.where(rank < 8, rank, rank + 8)
        at_odd = col * ROWS + jnp.where(rank < 8, rank + 8, rank + 12)
        onehot[g, :CELLS] = jnp.where(wide_lane == at_even, 1.0, 0.0).astype(jnp.bfloat16)
        onehot[g, CELLS:] = jnp.where(wide_lane == at_odd, 1.0, 0.0).astype(jnp.bfloat16)

    for dc in range(2):
        groups = [frame_at(dy, dc) for dy in range(4)]
        for g in groups:
            block = recv.at[pl.ds(g * NE, NE)]
            pltpu.make_async_copy(block, block, ret_recv.at[g]).wait()
        for g in groups:
            rows = recv[pl.ds(g * NE, NE)].astype(jnp.float32)
            rows = [rows[:, q * ROWS : (q + 1) * ROWS].reshape(NE * ROWS, 128) for q in range(3)]
            spectra[g] = nn(onehot[g], jnp.concatenate(rows, axis=1).astype(jnp.bfloat16))

    def products(i, carry):
        at = pl.multiple_of(i * 8, 8)
        total = [None] * 16
        for half in range(2):
            for k in range(3):
                pieces = [
                    spectra[g, pl.ds(at + half * CELLS, 8), k * 128 : (k + 1) * 128] for g in range(G)
                ]
                for s in range(4):
                    for q in range(4):
                        term = pieces[s] * pieces[4 + q]
                        n = s * 4 + q
                        total[n] = term if total[n] is None else total[n] + term
        for n in range(16):
            cross[n, pl.ds(at, 8), :] = total[n]
        return carry

    lax.fori_loop(0, CELLS // 8, products, 0, unroll=2)

    bank = filters_ref[...] * (1.0 / math.sqrt(NF))
    bank = jnp.concatenate([bank, bank], axis=1)
    bank_high = bank.astype(jnp.bfloat16)
    bank_low = (bank - bank_high.astype(jnp.float32)).astype(jnp.bfloat16)
    bank = jnp.concatenate([bank_high, bank_low], axis=0)
    bank = jnp.concatenate([bank, bank], axis=1)

    for p in range(PAIRS):
        value = cross[source_ref[p] * 4 + receiver_ref[p]]
        high = value.astype(jnp.bfloat16)
        low = (value - high.astype(jnp.float32)).astype(jnp.bfloat16)
        both = nt(bank, jnp.concatenate([high, low], axis=1))
        result[p] = both[:FILT] + both[FILT:]
        pltpu.make_async_copy(result.at[p], out_hbm.at[p], out_sem).start()

    pltpu.make_async_copy(result, out_hbm, out_sem).wait()
    others = pl.ds(0, G - 1)
    pltpu.make_async_copy(asked.at[others], asked.at[others], ask_send).wait()
    others = pl.ds(0, NE - 1)
    pltpu.make_async_copy(middle.at[:, others], middle.at[:, others], pass_send).wait()
    others = pl.ds(0, DEV - 1)
    pltpu.make_async_copy(send.at[others], send.at[others], ret_send).wait()


def local(strain_db, owner, local_elem, lattice, pair_source, pair_receiver, filters):
    hbm = pl.BlockSpec(memory_space=pltpu.HBM)
    database = jnp.transpose(strain_db[0], (1, 2, 0, 3))
    return pl.pallas_call(
        kernel,
        out_shape=jax.ShapeDtypeStruct((PAIRS, FILT, CELLS), jnp.float32),
        in_specs=[hbm] * 8,
        out_specs=hbm,
        scratch_shapes=[
            pltpu.VMEM((G, CELLS), jnp.int32),
            pltpu.VMEM((G, CELLS), jnp.int32),
            pltpu.VMEM((2 * G, CELLS), jnp.int32),
            pltpu.SMEM((PAIRS,), jnp.int32),
            pltpu.SMEM((PAIRS,), jnp.int32),
            pltpu.VMEM((FILT, NF), jnp.float32),
            pltpu.VMEM((T + DEV * CAP, 128), jnp.bfloat16),
            pltpu.VMEM((NP, 2, C, E, 128), jnp.bfloat16),
            pltpu.VMEM((C, NP * E, 128), jnp.bfloat16),
            pltpu.VMEM((G, NE, 1, 128), jnp.float32),
            pltpu.VMEM((G, NE, 1, 128), jnp.float32),
            pltpu.VMEM((G, NE, 1, 128), jnp.float32),
            pltpu.VMEM((NP, SLOTS, 128), jnp.bfloat16),
            pltpu.VMEM((NP, HALF * CAP, 128), jnp.bfloat16),
            pltpu.VMEM((NP, SLOTS, 128), jnp.bfloat16),
            pltpu.VMEM((DEV, 3 * ROWS, 128), jnp.bfloat16),
            pltpu.VMEM((DEV, 3 * ROWS, 128), jnp.bfloat16),
            pltpu.VMEM((G, 2 * CELLS, WIDE), jnp.bfloat16),
            pltpu.VMEM((G, 2 * CELLS, WIDE), jnp.float32),
            pltpu.VMEM((16, CELLS, 128), jnp.float32),
            pltpu.VMEM((PAIRS, FILT, CELLS), jnp.float32),
            pltpu.SemaphoreType.DMA((7,)),
            pltpu.SemaphoreType.DMA((NP // UNROLL,)),
            pltpu.SemaphoreType.DMA,
            pltpu.SemaphoreType.DMA,
            pltpu.SemaphoreType.DMA,
            pltpu.SemaphoreType.DMA,
            pltpu.SemaphoreType.DMA,
            pltpu.SemaphoreType.DMA((G,)),
            pltpu.SemaphoreType.DMA,
        ],
        compiler_params=pltpu.CompilerParams(
            collective_id=0, has_side_effects=True, vmem_limit_bytes=60 * 2**20
        ),
    )(
        database,
        owner.reshape(G, CELLS),
        local_elem,
        lattice.reshape(2 * G, CELLS),
        pair_source,
        pair_receiver,
        filters,
        jnp.asarray(constants()),
    )


def solution(mesh):
    placed = (
        P("frame", "elem", None, None, None),
        P(None, ("frame", "elem"), None),
        P(None, ("frame", "elem")),
        P(None, None, ("frame", "elem")),
        P(),
        P(),
        P(),
    )
    return jax.shard_map(
        local,
        mesh=mesh,
        in_specs=placed,
        out_specs=P(None, None, ("frame", "elem")),
        check_vma=False,
    )
```
